512 devices in a mesh: chol: 8 (over x, core), ao: 64 (over z, y).
Axes of the slice: x: 4, y: 4, z: 16, core: 2. Of those that a mesh axis runs over, the one named last changes fastest.
Arguments:
- cholesky: bfloat16 [32, 4096, 4096], P('chol', 'ao'), may hold values from -6 to 6
- orbitals: bfloat16 [4096, 256], replicated, may hold values from -0.09375 to 0.09375
- tile_pairs: int32 [64, 4, 2], P('ao'), may hold values from 0 to 255, as said below
Outputs:
- integrals: float32 [256, 256, 256], P('ao', 'chol')
The draws below stay inside these ranges and needn't reach their ends.
Inputs may be any that keep to these rules, and one draw needn't show every extreme that they name: `tile_pairs`: each pair has p <= r; every index of ao has 4 tiles.
All inputs are finite; a program needn't handle non-finite values.
Results may differ from the reference program's by a relative error of at most 0.0057.
Values may be sent and summed in bfloat16 or wider, within the bound.
A program may use at most 64 MiB of HBM per device.

```python
import jax
import jax.numpy as jnp
from jax import lax

NAO = 4096
NO = 256
TILES_DEV = 4
QV = 32
N_AO = 64


def draw_tile_pairs(key, part):
    key = jax.random.fold_in(key, 7)
    first_key, second_random_key = jax.random.split(key)
    first = jax.random.randint(first_key, (N_AO, TILES_DEV), 0, NO)
    first = first.at[0, 0].set(0)
    offset = jax.random.randint(second_random_key, (N_AO, TILES_DEV), 0, NO)
    second_operand = first + offset % (NO - first)
    second_operand = second_operand.at[N_AO - 1, TILES_DEV - 1].set(NO - 1)
    return jnp.stack([first, second_operand], axis=-1).astype(jnp.int32)


def steps_of(key, extent, cuts, low, largest):
    factor_of, own = 1.0, jax.random.fold_in(key, 6)
    for dim, shards_of in cuts:
        draws = jnp.exp(jax.random.uniform(jax.random.fold_in(own, dim), (shards_of,), jnp.float32, low / len(cuts), largest / len(cuts)))
        factor_of = factor_of * jnp.repeat(draws, extent[dim] // shards_of).reshape([-1 if axis == dim else 1 for axis in range(len(extent))])
    return factor_of


def normal_values(stream_key, dims, spread, reach, shards=(), dtype=jnp.bfloat16):
    result = spread * jax.random.normal(stream_key, dims, jnp.float32)
    if shards:
        result = result * steps_of(stream_key, dims, shards, -0.22, 0.18)
    return jnp.clip(result, -reach, reach).astype(dtype)


def setup_inputs(seed: int = 0) -> dict:
    keys = jax.random.split(jax.random.key(seed), 4)
    cholesky = normal_values(keys[0], (QV, NAO, NAO), 1.0, 6.0, ((0, 8), (1, 64)))
    orbitals = normal_values(keys[1], (NAO, NO), NAO ** -0.5, 0.09375)
    tile_pairs = draw_tile_pairs(jax.random.fold_in(keys[3], 71), 0)
    return {"cholesky": cholesky, "orbitals": orbitals, "tile_pairs": tile_pairs}


def reference(cholesky, orbitals, tile_pairs):
    def basis_change(slab):
        half = jnp.dot(slab, orbitals, preferred_element_type=jnp.float32).astype(jnp.bfloat16)
        return jnp.dot(orbitals.T, half, preferred_element_type=jnp.float32).astype(jnp.bfloat16)

    pair = lax.map(basis_change, cholesky)
    flat = tile_pairs.reshape(-1, 2)

    def one_tile(entry):
        left_factor = jnp.take(pair, entry[0], axis=1)
        right_factor = jnp.take(pair, entry[1], axis=1)
        return jnp.dot(left_factor.T, right_factor, preferred_element_type=jnp.float32)

    return lax.map(one_tile, flat)
```

```python
import jax
import jax.numpy as jnp
from jax import lax
from jax.experimental import pallas as pl
from jax.experimental.pallas import tpu as pltpu
from jax.sharding import PartitionSpec as P

MESH = pl.DeviceIdType.MESH
BF16, F32 = jnp.bfloat16, jnp.float32
GROUP = 16
QUADS = 4
CHOL = 8
CHUNKS = 4


def kernel(chol_hbm, orb_hbm, pairs_hbm, out_ref, chol_v, orb_v, pairs_s, acc, half_send, half_recv, orb_t,
           part_send, part_recv, index_send, index_recv, rows_send, rows_recv,
           load_sem, pairs_sem, half_sems, part_sems, index_sems, rows_sems):
    c, a = lax.axis_index("chol"), lax.axis_index("ao")
    quad, i = a // GROUP, a % GROUP
    base = quad * GROUP
    y, zl = i % 4, i // 4
    width = chol_v.shape[2] // CHUNKS

    loads = []
    for j in range(CHUNKS):
        cols = pl.ds(j * width, width)
        pair = (
            pltpu.make_async_copy(chol_hbm.at[:, :, cols], chol_v.at[:, :, cols], load_sem.at[0, j]),
            pltpu.make_async_copy(orb_hbm.at[cols, :], orb_v.at[cols, :], load_sem.at[1, j]),
        )
        for copy in pair:
            copy.start()
        loads.append(pair)
    pairs_copy = pltpu.make_async_copy(pairs_hbm, pairs_s, pairs_sem)
    pairs_copy.start()

    barrier = pltpu.get_barrier_semaphore()
    for d in range(1, QUADS):
        pl.semaphore_signal(barrier, 1, device_id=(c, (a + GROUP * d) % 64), device_id_type=MESH)
    for d in range(1, GROUP):
        pl.semaphore_signal(barrier, 1, device_id=(c, base + (i ^ d)), device_id_type=MESH)
    for d in range(1, CHOL):
        pl.semaphore_signal(barrier, 1, device_id=(c ^ d, a), device_id_type=MESH)

    lane = lambda rows: lax.broadcasted_iota(jnp.int32, (rows, 128), 1)
    row = lambda rows: lax.broadcasted_iota(jnp.int32, (rows, 128), 0)
    swap = lambda v: pltpu.roll(v, 64, axis=1)

    for j in range(CHUNKS):
        for copy in loads[j]:
            copy.wait()
        cols = pl.ds(j * width, width)
        term = jnp.dot(chol_v[:, :, cols].reshape(256, width), orb_v[cols, :], preferred_element_type=F32)
        acc[...] = term if j == 0 else acc[...] + term
    low32 = lane(32) < 64
    for k in range(4):
        for h in range(2):
            first = acc[k * 64 : k * 64 + 32, h * 128 : h * 128 + 128]
            second = acc[k * 64 + 32 : k * 64 + 64, h * 128 : h * 128 + 128]
            half_send[(2 * h) * 4 + k] = jnp.where(low32, first, swap(second)).astype(BF16)
            half_send[(2 * h + 1) * 4 + k] = jnp.where(low32, swap(first), second).astype(BF16)
    half_recv[i] = half_send[i]

    pairs_copy.wait()
    line = jnp.zeros((1, 128), F32)
    for t in range(4):
        for e in range(2):
            line = jnp.where(lane(1) == 2 * t + e, pairs_s[0, t, e].astype(F32), line)
    index_send[0] = line
    index_recv[i] = line

    pl.semaphore_wait(barrier, QUADS - 1 + GROUP - 1 + CHOL - 1)

    halves, indices = [], []
    for d in (10, 11, 9, 8, 14, 15, 13, 12, 6, 7, 5, 4, 2, 3, 1):
        to = (c, base + (i ^ d))
        halves.append(pltpu.make_async_remote_copy(
            half_send.at[i ^ d], half_recv.at[i], half_sems.at[0], half_sems.at[1], device_id=to, device_id_type=MESH))
        indices.append(pltpu.make_async_remote_copy(
            index_send.at[0], index_recv.at[i], index_sems.at[0], index_sems.at[1], device_id=to, device_id_type=MESH))
    for copy in halves:
        copy.start()
    for copy in indices:
        copy.start()

    eye = (lax.broadcasted_iota(jnp.int32, (256, 256), 0) == lax.broadcasted_iota(jnp.int32, (256, 256), 1)).astype(BF16)
    mine = orb_v[pl.ds(quad * 1024, 1024), :].reshape(16, 2, 32, 256)
    for h in range(2):
        orb_t[h] = lax.dot_general(
            eye, mine[:, h].reshape(512, 256), (((1,), (1,)), ((), ())), preferred_element_type=F32).astype(BF16)

    def wait_for(sem, ref):
        pltpu.make_async_copy(ref, ref, sem).wait()

    wait_for(half_sems.at[1], half_recv.at[pl.ds(0, GROUP - 1)])

    block = half_recv[...].reshape(512, 128)
    even = jnp.dot(orb_t[0], block, preferred_element_type=F32)
    odd = jnp.dot(orb_t[1], block, preferred_element_type=F32)
    own = jnp.where(lane(128) < 64, even[:128] + swap(odd[:128]), swap(even[128:]) + odd[128:])
    part_send[...] = own.astype(BF16)
    parts = []
    for d in (2, 1, 3):
        copy = pltpu.make_async_remote_copy(
            part_send, part_recv.at[d - 1], part_sems.at[0], part_sems.at[d],
            device_id=(c, (a + GROUP * d) % 64), device_id_type=MESH)
        copy.start()
        parts.append(copy)
    acc[:128, :128] = own

    wait_for(index_sems.at[1], index_recv.at[pl.ds(0, GROUP - 1)])
    table = jnp.broadcast_to(index_recv[...], (16, 4, 128)).reshape(64, 128)
    picks = []
    for e in range(2):
        column = jnp.sum(jnp.where(lane(64) == 2 * (row(64) % 4) + e, table, 0.0), axis=1, keepdims=True)
        picks.append(column.astype(jnp.int32))
    hot = lambda e, h: (picks[e] - 128 * h == lane(64)).astype(BF16)
    ones = jnp.concatenate([hot(0, 0), hot(1, 0), hot(0, 1), hot(1, 1)], axis=0)

    total = acc[:128, :128]
    for copy in parts:
        copy.wait_recv()
    for d in range(3):
        total = total + part_recv[d].astype(F32)
    chosen = jnp.dot(ones, total.astype(BF16), preferred_element_type=F32)
    message = jnp.where(
        lane(64) < 64, chosen[:64] + swap(chosen[128:192]), swap(chosen[64:128]) + chosen[192:256])
    rows_send[...] = message.reshape(16, 4, 128)
    slot = zl * 32 + y * 8 + c
    rows_recv[slot] = rows_send[i]

    def send(j, carry):
        d = 127 - j
        pltpu.make_async_remote_copy(
            rows_send.at[i ^ (d // 8)], rows_recv.at[slot], rows_sems.at[0], rows_sems.at[1],
            device_id=(c ^ (d % 8), base + (i ^ (d // 8))), device_id_type=MESH).start()
        return carry

    lax.fori_loop(0, 127, send, 0)
    for copy in parts:
        copy.wait_send()
    for copy in indices:
        copy.wait_send()
    wait_for(half_sems.at[0], half_recv.at[pl.ds(0, GROUP - 1)])
    wait_for(rows_sems.at[1], rows_recv.at[pl.ds(0, 127)])

    left = rows_recv[pl.ds((c // 2) * 32, 32)].reshape(128, 128)
    left = jnp.where(c % 2 == 0, left, pltpu.roll(left, 96, axis=1))
    wide = jnp.zeros((128, 128), F32)
    for t in range(4):
        moved = left if t == 0 else pltpu.roll(left, 32 * t, axis=1)
        wide = jnp.where((row(128) % 4 == t) & (lane(128) // 32 == t), moved, wide)
    wide = wide.astype(BF16)
    products = [
        lax.dot_general(wide, rows_recv[z * 32 : z * 32 + 32].reshape(128, 128).astype(BF16),
                        (((0,), (0,)), ((), ())), preferred_element_type=F32)
        for z in range(4)
    ]
    for h in range(2):
        joined = jnp.where(lane(128) < 64, swap(products[2 * h]), products[2 * h + 1])
        out_ref[:, :, h * 128 : h * 128 + 128] = joined.reshape(4, 32, 128)
    wait_for(rows_sems.at[0], rows_recv.at[pl.ds(0, 127)])


def on_device(cholesky, orbitals, tile_pairs):
    vmem, dma = pltpu.VMEM, pltpu.SemaphoreType.DMA
    return pl.pallas_call(
        kernel,
        out_shape=jax.ShapeDtypeStruct((4, 32, 256), F32),
        in_specs=[pl.BlockSpec(memory_space=pl.ANY)] * 3,
        out_specs=pl.BlockSpec(memory_space=pltpu.VMEM),
        scratch_shapes=[
            vmem(cholesky.shape, BF16),
            vmem(orbitals.shape, BF16),
            pltpu.SMEM(tile_pairs.shape, jnp.int32),
            vmem((256, 256), F32),
            vmem((16, 32, 128), BF16),
            vmem((16, 32, 128), BF16),
            vmem((2, 256, 512), BF16),
            vmem((128, 128), BF16),
            vmem((3, 128, 128), BF16),
            vmem((1, 1, 128), F32),
            vmem((16, 1, 128), F32),
            vmem((16, 4, 128), F32),
            vmem((128, 4, 128), F32),
            dma((2, CHUNKS)),
            dma,
            dma((2,)),
            dma((4,)),
            dma((2,)),
            dma((2,)),
        ],
        compiler_params=pltpu.CompilerParams(
            collective_id=0, has_side_effects=True, vmem_limit_bytes=48 * 2**20),
        cost_estimate=pl.CostEstimate(flops=700_000_000, bytes_accessed=4_400_000, transcendentals=0),
    )(cholesky, orbitals, tile_pairs)


def solution(mesh):
    return jax.shard_map(
        on_device,
        mesh=mesh,
        in_specs=(P("chol", "ao", None), P(), P("ao", None, None)),
        out_specs=P("ao", "chol", None),
        check_vma=False,
    )
```

```python
import jax
import jax.numpy as jnp
from jax import lax
from jax.experimental import pallas as pl
from jax.experimental.pallas import tpu as pltpu
from jax.sharding import PartitionSpec as P

MESH = pl.DeviceIdType.MESH
BF16, F32 = jnp.bfloat16, jnp.float32
GROUP = 16
QUADS = 4
CHOL = 8
CHUNKS = 4
SHIFT = 8


def kernel(chol_hbm, orb_hbm, pairs_hbm, out_ref, chol_v, orb_v, pairs_s, acc, half_send, half_recv, orb_t,
           part_send, part_recv, index_send, index_recv, rows_send, rows_recv,
           load_sem, pairs_sem, half_sems, part_sems, index_sems, rows_sems):
    c, a = lax.axis_index("chol"), lax.axis_index("ao")
    shifted = (a + SHIFT) & 63
    quad, i = shifted >> 4, shifted & 15
    flip = 12 * (quad >> 1)
    block = i ^ flip

    def member(place):
        return (quad * GROUP + place - SHIFT) & 63

    def same_block(d):
        other = (quad + d) & 3
        return (other * GROUP + (block ^ (12 * (other >> 1))) - SHIFT) & 63

    width = chol_v.shape[2] // CHUNKS

    loads = []
    for j in range(CHUNKS):
        cols = pl.ds(j * width, width)
        pair = (
            pltpu.make_async_copy(chol_hbm.at[:, :, cols], chol_v.at[:, :, cols], load_sem.at[0, j]),
            pltpu.make_async_copy(orb_hbm.at[cols, :], orb_v.at[cols, :], load_sem.at[1, j]),
        )
        for copy in pair:
            copy.start()
        loads.append(pair)
    pairs_copy = pltpu.make_async_copy(pairs_hbm, pairs_s, pairs_sem)
    pairs_copy.start()

    barrier = pltpu.get_barrier_semaphore()
    for d in range(1, QUADS):
        pl.semaphore_signal(barrier, 1, device_id=(c, same_block(d)), device_id_type=MESH)
    for d in range(1, GROUP):
        pl.semaphore_signal(barrier, 1, device_id=(c, member(i ^ d)), device_id_type=MESH)
    for d in range(1, CHOL):
        pl.semaphore_signal(barrier, 1, device_id=(c ^ d, a), device_id_type=MESH)

    lane = lambda rows: lax.broadcasted_iota(jnp.int32, (rows, 128), 1)
    row = lambda rows: lax.broadcasted_iota(jnp.int32, (rows, 128), 0)
    swap = lambda v: pltpu.roll(v, 64, axis=1)

    for j in range(CHUNKS):
        for copy in loads[j]:
            copy.wait()
        cols = pl.ds(j * width, width)
        term = jnp.dot(chol_v[:, :, cols].reshape(256, width), orb_v[cols, :], preferred_element_type=F32)
        acc[...] = term if j == 0 else acc[...] + term
    low32 = lane(32) < 64
    for k in range(4):
        for h in range(2):
            first = acc[k * 64 : k * 64 + 32, h * 128 : h * 128 + 128]
            second = acc[k * 64 + 32 : k * 64 + 64, h * 128 : h * 128 + 128]
            half_send[(2 * h) * 4 + k] = jnp.where(low32, first, swap(second)).astype(BF16)
            half_send[(2 * h + 1) * 4 + k] = jnp.where(low32, swap(first), second).astype(BF16)
    half_recv[i] = half_send[block]

    pairs_copy.wait()
    line = jnp.zeros((1, 128), F32)
    for t in range(4):
        for e in range(2):
            line = jnp.where(lane(1) == 2 * t + e, pairs_s[0, e, t].astype(F32), line)
    index_send[0] = line
    index_recv[i] = line

    pl.semaphore_wait(barrier, QUADS - 1 + GROUP - 1 + CHOL - 1)

    halves, indices = [], []
    for d in (10, 11, 9, 8, 14, 15, 13, 12, 6, 7, 5, 4, 2, 3, 1):
        to = (c, member(i ^ d))
        halves.append(pltpu.make_async_remote_copy(
            half_send.at[block ^ d], half_recv.at[i], half_sems.at[0], half_sems.at[1], device_id=to, device_id_type=MESH))
        indices.append(pltpu.make_async_remote_copy(
            index_send.at[0], index_recv.at[i], index_sems.at[0], index_sems.at[1], device_id=to, device_id_type=MESH))
    for copy in halves + indices:
        copy.start()

    eye = (lax.broadcasted_iota(jnp.int32, (256, 256), 0) == lax.broadcasted_iota(jnp.int32, (256, 256), 1)).astype(BF16)
    for z in range(4):
        start = ((quad * GROUP + 4 * z - SHIFT) & 63) * 64
        mine = orb_v[pl.ds(pl.multiple_of(start, 256), 256), :].reshape(4, 2, 32, 256)
        for h in range(2):
            orb_t[h, :, z * 128 : z * 128 + 128] = lax.dot_general(
                eye, mine[:, h].reshape(128, 256), (((1,), (1,)), ((), ())), preferred_element_type=F32).astype(BF16)

    def wait_for(sem, ref):
        pltpu.make_async_copy(ref, ref, sem).wait()

    wait_for(half_sems.at[1], half_recv.at[pl.ds(0, GROUP - 1)])

    rows = half_recv[...].reshape(512, 128)
    even = jnp.dot(orb_t[0], rows, preferred_element_type=F32)
    odd = jnp.dot(orb_t[1], rows, preferred_element_type=F32)
    own = jnp.where(lane(128) < 64, even[:128] + swap(odd[:128]), swap(even[128:]) + odd[128:])
    part_send[...] = own.astype(BF16)
    parts = []
    for d in (2, 1, 3):
        copy = pltpu.make_async_remote_copy(
            part_send, part_recv.at[d - 1], part_sems.at[0], part_sems.at[d],
            device_id=(c, same_block(d)), device_id_type=MESH)
        copy.start()
        parts.append(copy)
    acc[:128, :128] = own

    wait_for(index_sems.at[1], index_recv.at[pl.ds(0, GROUP - 1)])
    table = jnp.broadcast_to(index_recv[...], (16, 4, 128)).reshape(64, 128)
    picks = []
    for e in range(2):
        column = jnp.sum(jnp.where(lane(64) == 2 * (row(64) % 4) + e, table, 0.0), axis=1, keepdims=True)
        picks.append(column.astype(jnp.int32))
    hot = lambda e, h: (picks[e] - 128 * h == lane(64)).astype(BF16)
    ones = jnp.concatenate([hot(0, 0), hot(1, 0), hot(0, 1), hot(1, 1)], axis=0)

    total = acc[:128, :128]
    for copy in parts:
        copy.wait_recv()
    for d in range(3):
        total = total + part_recv[d].astype(F32)
    chosen = jnp.dot(ones, total.astype(BF16), preferred_element_type=F32)
    message = jnp.where(
        lane(64) < 64, chosen[:64] + swap(chosen[128:192]), swap(chosen[64:128]) + chosen[192:256])
    rows_send[...] = message.astype(BF16).reshape(16, 4, 128)
    slot = block * 8 + c
    rows_recv[slot] = rows_send[i]

    def send(place, f):
        pltpu.make_async_remote_copy(
            rows_send.at[place], rows_recv.at[slot], rows_sems.at[0], rows_sems.at[1],
            device_id=(c ^ f, member(place)), device_id_type=MESH).start()

    def send_member(j, carry):
        for f in (4, 5, 6, 7, 2, 3, 0, 1):
            send(i ^ (15 - j), f)
        return carry

    lax.fori_loop(0, 15, send_member, 0)
    for f in (4, 5, 6, 7, 2, 3, 1):
        send(i, f)
    for copy in parts:
        copy.wait_send()
    for copy in indices:
        copy.wait_send()
    wait_for(half_sems.at[0], half_recv.at[pl.ds(0, GROUP - 1)])
    wait_for(rows_sems.at[1], rows_recv.at[pl.ds(0, 127)])

    left = rows_recv[pl.ds((c >> 1) * 32, 32)].reshape(128, 128).astype(F32)
    left = jnp.where((c & 1) == 0, left, pltpu.roll(left, 96, axis=1))
    wide = jnp.zeros((128, 128), F32)
    for t in range(4):
        moved = left if t == 0 else pltpu.roll(left, 32 * t, axis=1)
        wide = jnp.where((row(128) % 4 == t) & (lane(128) // 32 == t), moved, wide)
    wide = wide.astype(BF16)
    products = [
        lax.dot_general(wide, rows_recv[z * 32 : z * 32 + 32].reshape(128, 128),
                        (((0,), (0,)), ((), ())), preferred_element_type=F32)
        for z in range(4)
    ]
    for h in range(2):
        joined = jnp.where(lane(128) < 64, swap(products[2 * h]), products[2 * h + 1])
        out_ref[:, :, h * 128 : h * 128 + 128] = joined.reshape(4, 32, 128)
    wait_for(rows_sems.at[0], rows_recv.at[pl.ds(0, 127)])


def on_device(cholesky, orbitals, tile_pairs):
    vmem, dma = pltpu.VMEM, pltpu.SemaphoreType.DMA
    return pl.pallas_call(
        kernel,
        out_shape=jax.ShapeDtypeStruct((4, 32, 256), F32),
        in_specs=[pl.BlockSpec(memory_space=pltpu.HBM)] * 3,
        out_specs=pl.BlockSpec(memory_space=pltpu.VMEM),
        scratch_shapes=[
            vmem(cholesky.shape, BF16),
            vmem(orbitals.shape, BF16),
            pltpu.SMEM((1, 2, 4), jnp.int32),
            vmem((256, 256), F32),
            vmem((16, 32, 128), BF16),
            vmem((16, 32, 128), BF16),
            vmem((2, 256, 512), BF16),
            vmem((128, 128), BF16),
            vmem((3, 128, 128), BF16),
            vmem((1, 1, 128), F32),
            vmem((16, 1, 128), F32),
            vmem((16, 4, 128), BF16),
            vmem((128, 4, 128), BF16),
            dma((2, CHUNKS)),
            dma,
            dma((2,)),
            dma((4,)),
            dma((2,)),
            dma((2,)),
        ],
        compiler_params=pltpu.CompilerParams(
            collective_id=0, has_side_effects=True, vmem_limit_bytes=60 * 2**20),
        cost_estimate=pl.CostEstimate(flops=700_000_000, bytes_accessed=4_400_000, transcendentals=0),
    )(cholesky, orbitals, jnp.swapaxes(tile_pairs, 1, 2))


def solution(mesh):
    return jax.shard_map(
        on_device,
        mesh=mesh,
        in_specs=(P("chol", "ao", None), P(), P("ao", None, None)),
        out_specs=P("ao", "chol", None),
        check_vma=False,
    )
```

```python
import jax
import jax.numpy as jnp
from jax import lax
from jax.experimental import pallas as pl
from jax.experimental.pallas import tpu as pltpu
from jax.sharding import PartitionSpec as P

MESH = pl.DeviceIdType.MESH
BF16, F32 = jnp.bfloat16, jnp.float32
GROUP = 16
QUADS = 4
CHOL = 8
CHUNKS = 4


def kernel(chol_hbm, orb_hbm, pairs_hbm, out_ref, chol_v, orb_v, pairs_s, acc, half_send, half_recv, orb_t,
           part_send, part_recv, index_send, index_recv, rows_send, rows_recv,
           load_sem, pairs_sem, half_sems, part_sems, index_sems, rows_sems):
    c, a = lax.axis_index("chol"), lax.axis_index("ao")
    quad, i = a >> 4, a & 15
    flip = 12 * (quad >> 1)
    block = i ^ flip

    def member(place):
        return quad * GROUP + place

    def same_block(d):
        other = (quad + d) & 3
        return other * GROUP + (block ^ (12 * (other >> 1)))

    width = chol_v.shape[2] // CHUNKS

    barrier = pltpu.get_barrier_semaphore()
    for d in (2, 1, 3):
        pl.semaphore_signal(barrier, 1, device_id=(c, same_block(d)), device_id_type=MESH)
    for d in (10, 11, 9, 8, 14, 15, 13, 12, 6, 7, 5, 4, 2, 3, 1):
        pl.semaphore_signal(barrier, 1, device_id=(c, member(i ^ d)), device_id_type=MESH)
    for d in (4, 5, 6, 7, 2, 3, 1):
        pl.semaphore_signal(barrier, 1, device_id=(c ^ d, a), device_id_type=MESH)

    loads = []
    for j in range(CHUNKS):
        cols = pl.ds(j * width, width)
        pair = (
            pltpu.make_async_copy(chol_hbm.at[:, :, cols], chol_v.at[:, :, cols], load_sem.at[0, j]),
            pltpu.make_async_copy(orb_hbm.at[cols, :], orb_v.at[cols, :], load_sem.at[1, j]),
        )
        for copy in pair:
            copy.start()
        loads.append(pair)
    pairs_copy = pltpu.make_async_copy(pairs_hbm, pairs_s, pairs_sem)
    pairs_copy.start()

    lane = lambda rows: lax.broadcasted_iota(jnp.int32, (rows, 128), 1)
    row = lambda rows: lax.broadcasted_iota(jnp.int32, (rows, 128), 0)
    swap = lambda v: pltpu.roll(v, 64, axis=1)

    for j in range(CHUNKS):
        for copy in loads[j]:
            copy.wait()
        cols = pl.ds(j * width, width)
        term = jnp.dot(chol_v[:, :, cols].reshape(256, width), orb_v[cols, :], preferred_element_type=F32)
        acc[...] = term if j == 0 else acc[...] + term
    low32 = lane(32) < 64
    for k in range(4):
        for h in range(2):
            first = acc[k * 64 : k * 64 + 32, h * 128 : h * 128 + 128]
            second = acc[k * 64 + 32 : k * 64 + 64, h * 128 : h * 128 + 128]
            half_send[(2 * h) * 4 + k] = jnp.where(low32, first, swap(second)).astype(BF16)
            half_send[(2 * h + 1) * 4 + k] = jnp.where(low32, swap(first), second).astype(BF16)
    half_recv[i] = half_send[block]

    pairs_copy.wait()
    line = jnp.zeros((1, 128), F32)
    for t in range(4):
        for e in range(2):
            line = jnp.where(lane(1) == 2 * t + e, pairs_s[0, e, t].astype(F32), line)
    index_send[0] = line
    index_recv[i] = line

    pl.semaphore_wait(barrier, QUADS - 1 + GROUP - 1 + CHOL - 1)

    halves, indices = [], []
    for d in (10, 11, 9, 8, 14, 15, 13, 12, 6, 7, 5, 4, 2, 3, 1):
        to = (c, member(i ^ d))
        halves.append(pltpu.make_async_remote_copy(
            half_send.at[block ^ d], half_recv.at[i], half_sems.at[0], half_sems.at[1], device_id=to, device_id_type=MESH))
        indices.append(pltpu.make_async_remote_copy(
            index_send.at[0], index_recv.at[i], index_sems.at[0], index_sems.at[1], device_id=to, device_id_type=MESH))
    for copy in halves + indices:
        copy.start()

    eye = (lax.broadcasted_iota(jnp.int32, (256, 256), 0) == lax.broadcasted_iota(jnp.int32, (256, 256), 1)).astype(BF16)
    for z in range(4):
        start = (quad * GROUP + 4 * z) * 64
        mine = orb_v[pl.ds(pl.multiple_of(start, 256), 256), :].reshape(4, 2, 32, 256)
        for h in range(2):
            orb_t[h, :, z * 128 : z * 128 + 128] = lax.dot_general(
                eye, mine[:, h].reshape(128, 256), (((1,), (1,)), ((), ())), preferred_element_type=F32).astype(BF16)

    def wait_for(sem, ref):
        pltpu.make_async_copy(ref, ref, sem).wait()

    wait_for(half_sems.at[1], half_recv.at[pl.ds(0, GROUP - 1)])

    rows = half_recv[...].reshape(512, 128)
    even = jnp.dot(orb_t[0], rows, preferred_element_type=F32)
    odd = jnp.dot(orb_t[1], rows, preferred_element_type=F32)
    own = jnp.where(lane(128) < 64, even[:128] + swap(odd[:128]), swap(even[128:]) + odd[128:])
    part_send[...] = own.astype(BF16)
    parts = []
    for d in (2, 1, 3):
        copy = pltpu.make_async_remote_copy(
            part_send, part_recv.at[d - 1], part_sems.at[0], part_sems.at[d],
            device_id=(c, same_block(d)), device_id_type=MESH)
        copy.start()
        parts.append(copy)
    acc[:128, :128] = own

    wait_for(index_sems.at[1], index_recv.at[pl.ds(0, GROUP - 1)])
    table = jnp.broadcast_to(index_recv[...], (16, 4, 128)).reshape(64, 128)
    picks = []
    for e in range(2):
        column = jnp.sum(jnp.where(lane(64) == 2 * (row(64) % 4) + e, table, 0.0), axis=1, keepdims=True)
        picks.append(column.astype(jnp.int32))
    hot = lambda e, h: (picks[e] - 128 * h == lane(64)).astype(BF16)
    ones = jnp.concatenate([hot(0, 0), hot(1, 0), hot(0, 1), hot(1, 1)], axis=0)

    total = acc[:128, :128]
    for copy in parts:
        copy.wait_recv()
    for d in range(3):
        total = total + part_recv[d].astype(F32)
    chosen = jnp.dot(ones, total.astype(BF16), preferred_element_type=F32)
    message = jnp.where(
        lane(64) < 64, chosen[:64] + swap(chosen[128:192]), swap(chosen[64:128]) + chosen[192:256])
    rows_send[...] = message.astype(BF16).reshape(16, 4, 128)
    slot = block * 8 + c
    rows_recv[slot] = rows_send[i]

    def send(place, f):
        pltpu.make_async_remote_copy(
            rows_send.at[place], rows_recv.at[slot], rows_sems.at[0], rows_sems.at[1],
            device_id=(c ^ f, member(place)), device_id_type=MESH).start()

    def send_member(j, carry):
        for f in (4, 5, 6, 7, 2, 3, 0, 1):
            send(i ^ (15 - j), f)
        return carry

    lax.fori_loop(0, 15, send_member, 0)
    for f in (4, 5, 6, 7, 2, 3, 1):
        send(i, f)
    for copy in parts:
        copy.wait_send()
    for copy in indices:
        copy.wait_send()
    wait_for(half_sems.at[0], half_recv.at[pl.ds(0, GROUP - 1)])
    wait_for(rows_sems.at[1], rows_recv.at[pl.ds(0, 127)])

    left = rows_recv[pl.ds((c >> 1) * 32, 32)].reshape(128, 128).astype(F32)
    left = jnp.where((c & 1) == 0, left, pltpu.roll(left, 96, axis=1))
    wide = jnp.zeros((128, 128), F32)
    for t in range(4):
        moved = left if t == 0 else pltpu.roll(left, 32 * t, axis=1)
        wide = jnp.where((row(128) % 4 == t) & (lane(128) // 32 == t), moved, wide)
    wide = wide.astype(BF16)
    products = [
        lax.dot_general(wide, rows_recv[z * 32 : z * 32 + 32].reshape(128, 128),
                        (((0,), (0,)), ((), ())), preferred_element_type=F32)
        for z in range(4)
    ]
    for h in range(2):
        joined = jnp.where(lane(128) < 64, swap(products[2 * h]), products[2 * h + 1])
        out_ref[:, :, h * 128 : h * 128 + 128] = joined.reshape(4, 32, 128)
    wait_for(rows_sems.at[0], rows_recv.at[pl.ds(0, 127)])


def on_device(cholesky, orbitals, tile_pairs):
    vmem, dma = pltpu.VMEM, pltpu.SemaphoreType.DMA
    return pl.pallas_call(
        kernel,
        out_shape=jax.ShapeDtypeStruct((4, 32, 256), F32),
        in_specs=[pl.BlockSpec(memory_space=pltpu.HBM)] * 3,
        out_specs=pl.BlockSpec(memory_space=pltpu.VMEM),
        scratch_shapes=[
            vmem(cholesky.shape, BF16),
            vmem(orbitals.shape, BF16),
            pltpu.SMEM((1, 2, 4), jnp.int32),
            vmem((256, 256), F32),
            vmem((16, 32, 128), BF16),
            vmem((16, 32, 128), BF16),
            vmem((2, 256, 512), BF16),
            vmem((128, 128), BF16),
            vmem((3, 128, 128), BF16),
            vmem((1, 1, 128), F32),
            vmem((16, 1, 128), F32),
            vmem((16, 4, 128), BF16),
            vmem((128, 4, 128), BF16),
            dma((2, CHUNKS)),
            dma,
            dma((2,)),
            dma((4,)),
            dma((2,)),
            dma((2,)),
        ],
        compiler_params=pltpu.CompilerParams(
            collective_id=0, has_side_effects=True, vmem_limit_bytes=53 * 2**20),
        cost_estimate=pl.CostEstimate(flops=700_000_000, bytes_accessed=4_400_000, transcendentals=0),
    )(cholesky, orbitals, pltpu.with_memory_space_constraint(jnp.swapaxes(tile_pairs, 1, 2), pltpu.HBM))


def solution(mesh):
    return jax.shard_map(
        on_device,
        mesh=mesh,
        in_specs=(P("chol", "ao", None), P(), P("ao", None, None)),
        out_specs=P("ao", "chol", None),
        check_vma=False,
    )
```

```python
import jax
import jax.numpy as jnp
from jax import lax
from jax.experimental import pallas as pl
from jax.experimental.pallas import tpu as pltpu
from jax.sharding import PartitionSpec as P

MESH = pl.DeviceIdType.MESH
BF16, F32 = jnp.bfloat16, jnp.float32
GROUP = 16
QUADS = 4
CHOL = 8
CHUNKS = 4


def kernel(chol_hbm, orb_hbm, pairs_hbm, out_ref, chol_v, orb_v, pairs_s, acc, half_send, half_recv, orb_t,
           part_send, part_sum, part_recv, index_send, index_recv, rows_send, rows_recv,
           load_sem, pairs_sem, half_sems, part_sems, index_sems, rows_sems):
    c, a = lax.axis_index("chol"), lax.axis_index("ao")
    quad, i = a >> 4, a & 15

    def turned(q, place):
        far = q >> 1
        return (((1 - 2 * far) * (place >> 2) + 3 * far * (1 - (q & 1))) & 3) * 4 + (place & 3)

    block = turned(quad, i)

    def member(place):
        return quad * GROUP + place

    def same_block(d):
        other = (quad + d) & 3
        return other * GROUP + turned(other, block)

    width = chol_v.shape[2] // CHUNKS

    barrier = pltpu.get_barrier_semaphore()
    for d in (2, 1, 3):
        pl.semaphore_signal(barrier, 1, device_id=(c, same_block(d)), device_id_type=MESH)
    for d in (10, 11, 9, 8, 14, 15, 13, 12, 6, 7, 5, 4, 2, 3, 1):
        pl.semaphore_signal(barrier, 1, device_id=(c, member(i ^ d)), device_id_type=MESH)
    for d in (4, 5, 6, 7, 2, 3, 1):
        pl.semaphore_signal(barrier, 1, device_id=(c ^ d, a), device_id_type=MESH)

    loads = []
    for j in range(CHUNKS):
        cols = pl.ds(j * width, width)
        pair = (
            pltpu.make_async_copy(chol_hbm.at[:, :, cols], chol_v.at[:, :, cols], load_sem.at[0, j]),
            pltpu.make_async_copy(orb_hbm.at[cols, :], orb_v.at[cols, :], load_sem.at[1, j]),
        )
        for copy in pair:
            copy.start()
        loads.append(pair)
    pairs_copy = pltpu.make_async_copy(pairs_hbm, pairs_s, pairs_sem)
    pairs_copy.start()

    lane = lambda rows: lax.broadcasted_iota(jnp.int32, (rows, 128), 1)
    row = lambda rows: lax.broadcasted_iota(jnp.int32, (rows, 128), 0)
    swap = lambda v: pltpu.roll(v, 64, axis=1)

    for j in range(CHUNKS):
        for copy in loads[j]:
            copy.wait()
        cols = pl.ds(j * width, width)
        term = jnp.dot(chol_v[:, :, cols].reshape(256, width), orb_v[cols, :], preferred_element_type=F32)
        acc[...] = term if j == 0 else acc[...] + term
    low32 = lane(32) < 64
    for k in range(4):
        for h in range(2):
            first = acc[k * 64 : k * 64 + 32, h * 128 : h * 128 + 128]
            second = acc[k * 64 + 32 : k * 64 + 64, h * 128 : h * 128 + 128]
            half_send[(2 * h) * 4 + k] = jnp.where(low32, first, swap(second)).astype(BF16)
            half_send[(2 * h + 1) * 4 + k] = jnp.where(low32, swap(first), second).astype(BF16)
    half_recv[i] = half_send[block]

    pairs_copy.wait()
    line = jnp.zeros((1, 128), F32)
    for t in range(4):
        for e in range(2):
            line = jnp.where(lane(1) == 2 * t + e, pairs_s[0, e, t].astype(F32), line)
    index_send[0] = line
    index_recv[i] = line

    @pl.when(quad == 1)
    def _():
        part_recv[1] = jnp.zeros((128, 128), BF16)

    pl.semaphore_wait(barrier, QUADS - 1 + GROUP - 1 + CHOL - 1)

    halves, indices = [], []
    for d in (10, 11, 9, 8, 14, 15, 13, 12, 6, 7, 5, 4, 2, 3, 1):
        to = (c, member(i ^ d))
        halves.append(pltpu.make_async_remote_copy(
            half_send.at[turned(quad, i ^ d)], half_recv.at[i], half_sems.at[0], half_sems.at[1], device_id=to, device_id_type=MESH))
        indices.append(pltpu.make_async_remote_copy(
            index_send.at[0], index_recv.at[i], index_sems.at[0], index_sems.at[1], device_id=to, device_id_type=MESH))
    for copy in halves + indices:
        copy.start()

    eye = (lax.broadcasted_iota(jnp.int32, (256, 256), 0) == lax.broadcasted_iota(jnp.int32, (256, 256), 1)).astype(BF16)
    for z in range(4):
        start = (quad * GROUP + 4 * z) * 64
        mine = orb_v[pl.ds(pl.multiple_of(start, 256), 256), :].reshape(4, 2, 32, 256)
        for h in range(2):
            orb_t[h, :, z * 128 : z * 128 + 128] = lax.dot_general(
                eye, mine[:, h].reshape(128, 256), (((1,), (1,)), ((), ())), preferred_element_type=F32).astype(BF16)

    def wait_for(sem, ref):
        pltpu.make_async_copy(ref, ref, sem).wait()

    wait_for(half_sems.at[1], half_recv.at[pl.ds(0, GROUP - 1)])

    rows = half_recv[...].reshape(512, 128)
    even = jnp.dot(orb_t[0], rows, preferred_element_type=F32)
    odd = jnp.dot(orb_t[1], rows, preferred_element_type=F32)
    own = jnp.where(lane(128) < 64, even[:128] + swap(odd[:128]), swap(even[128:]) + odd[128:])
    part_send[...] = own.astype(BF16)

    def part(d, source):
        return pltpu.make_async_remote_copy(
            source, part_recv.at[d - 1], part_sems.at[0], part_sems.at[d],
            device_id=(c, same_block(d)), device_id_type=MESH)

    @pl.when(quad != 3)
    def _():
        part(2, part_send).start()

    @pl.when(quad != 0)
    def _():
        part(1, part_send).start()

    part(3, part_send).start()
    acc[:128, :128] = own

    wait_for(index_sems.at[1], index_recv.at[pl.ds(0, GROUP - 1)])
    table = jnp.broadcast_to(index_recv[...], (16, 4, 128)).reshape(64, 128)
    picks = []
    for e in range(2):
        column = jnp.sum(jnp.where(lane(64) == 2 * (row(64) % 4) + e, table, 0.0), axis=1, keepdims=True)
        picks.append(column.astype(jnp.int32))
    hot = lambda e, h: (picks[e] - 128 * h == lane(64)).astype(BF16)
    ones = jnp.concatenate([hot(0, 0), hot(1, 0), hot(0, 1), hot(1, 1)], axis=0)

    total = acc[:128, :128]
    part(1, part_send).wait_recv()
    total = total + part_recv[0].astype(F32)

    @pl.when(quad == 0)
    def _():
        part_sum[...] = total.astype(BF16)
        part(1, part_sum).start()

    part(3, part_send).wait_recv()

    @pl.when(quad != 1)
    def _():
        part(2, part_send).wait_recv()

    total = total + part_recv[1].astype(F32) + part_recv[2].astype(F32)
    chosen = jnp.dot(ones, total.astype(BF16), preferred_element_type=F32)
    message = jnp.where(
        lane(64) < 64, chosen[:64] + swap(chosen[128:192]), swap(chosen[64:128]) + chosen[192:256])
    rows_send[...] = message.astype(BF16).reshape(16, 4, 128)
    slot = block * 8 + c
    rows_recv[slot] = rows_send[i]

    def send(place, f):
        pltpu.make_async_remote_copy(
            rows_send.at[place], rows_recv.at[slot], rows_sems.at[0], rows_sems.at[1],
            device_id=(c ^ f, member(place)), device_id_type=MESH).start()

    def send_member(j, carry):
        for f in (4, 5, 6, 7, 2, 3, 0, 1):
            send(j + (j >= i).astype(jnp.int32), f)
        return carry

    lax.fori_loop(0, 15, send_member, 0)
    for f in (4, 5, 6, 7, 2, 3, 1):
        send(i, f)
    part(1, part_send).wait_send()
    part(3, part_send).wait_send()

    @pl.when(quad != 3)
    def _():
        part(2, part_send).wait_send()

    for copy in indices:
        copy.wait_send()
    wait_for(half_sems.at[0], half_recv.at[pl.ds(0, GROUP - 1)])
    wait_for(rows_sems.at[1], rows_recv.at[pl.ds(0, 127)])

    left = rows_recv[pl.ds((c >> 1) * 32, 32)].reshape(128, 128).astype(F32)
    left = jnp.where((c & 1) == 0, left, pltpu.roll(left, 96, axis=1))
    wide = jnp.zeros((128, 128), F32)
    for t in range(4):
        moved = left if t == 0 else pltpu.roll(left, 32 * t, axis=1)
        wide = jnp.where((row(128) % 4 == t) & (lane(128) // 32 == t), moved, wide)
    wide = wide.T.astype(BF16)
    products = [
        jnp.dot(wide, rows_recv[z * 32 : z * 32 + 32].reshape(128, 128), preferred_element_type=F32)
        for z in range(4)
    ]
    for h in range(2):
        joined = jnp.where(lane(128) < 64, swap(products[2 * h]), products[2 * h + 1])
        out_ref[:, :, h * 128 : h * 128 + 128] = joined.reshape(4, 32, 128)
    wait_for(rows_sems.at[0], rows_recv.at[pl.ds(0, 127)])


def on_device(cholesky, orbitals, tile_pairs):
    vmem, dma = pltpu.VMEM, pltpu.SemaphoreType.DMA
    return pl.pallas_call(
        kernel,
        out_shape=jax.ShapeDtypeStruct((4, 32, 256), F32),
        in_specs=[pl.BlockSpec(memory_space=pltpu.HBM)] * 3,
        out_specs=pl.BlockSpec(memory_space=pltpu.VMEM),
        scratch_shapes=[
            vmem(cholesky.shape, BF16),
            vmem(orbitals.shape, BF16),
            pltpu.SMEM((1, 2, 4), jnp.int32),
            vmem((256, 256), F32),
            vmem((16, 32, 128), BF16),
            vmem((16, 32, 128), BF16),
            vmem((2, 256, 512), BF16),
            vmem((128, 128), BF16),
            vmem((128, 128), BF16),
            vmem((3, 128, 128), BF16),
            vmem((1, 1, 128), F32),
            vmem((16, 1, 128), F32),
            vmem((16, 4, 128), BF16),
            vmem((128, 4, 128), BF16),
            dma((2, CHUNKS)),
            dma,
            dma((2,)),
            dma((4,)),
            dma((2,)),
            dma((2,)),
        ],
        compiler_params=pltpu.CompilerParams(
            collective_id=0, has_side_effects=True, vmem_limit_bytes=53 * 2**20),
        cost_estimate=pl.CostEstimate(flops=700_000_000, bytes_accessed=4_400_000, transcendentals=0),
    )(cholesky, orbitals, pltpu.with_memory_space_constraint(jnp.swapaxes(tile_pairs, 1, 2), pltpu.HBM))


def solution(mesh):
    return jax.shard_map(
        on_device,
        mesh=mesh,
        in_specs=(P("chol", "ao", None), P(), P("ao", None, None)),
        out_specs=P("ao", "chol", None),
        check_vma=False,
    )
```
